32 devices in a mesh: ctx: 8 (over y, x, core), head: 4 (over z).
Axes of the slice: x: 2, y: 2, z: 4, core: 2. Of those that a mesh axis runs over, the one named last changes fastest.
Arguments:
- q_att: bfloat16 [2048, 512], P('ctx', 'head'), may hold values from -6 to 6
- k_att: bfloat16 [2048, 512], P('ctx', 'head'), may hold values from -6 to 6
- v_att: bfloat16 [2048, 512], P('ctx', 'head'), may hold values from -6 to 6
- norm_gain: float32 [512], P('head'), may hold values from 0.25 to 1.75
- hy_q: bfloat16 [2048, 512], P('ctx', 'head'), may hold values from -6 to 6
- hy_k: bfloat16 [2048, 512], P('ctx', 'head'), may hold values from -6 to 6
- feat_w: float32 [3, 7, 512], P(None, None, 'head'), may hold values from -2 to 2
- mr_filt: float32 [128, 32], P(None, 'head'), may hold values from -0.5 to 0.5
- cotangent: bfloat16 [2048, 512], P('ctx', 'head'), may hold values from -6 to 6
Outputs:
- output: bfloat16 [2048, 512], P('ctx', 'head')
- grad_q: bfloat16 [2048, 512], P('ctx', 'head')
- grad_k: bfloat16 [2048, 512], P('ctx', 'head')
- grad_v: bfloat16 [2048, 512], P('ctx', 'head')
The draws below stay inside these ranges and needn't reach their ends.
All inputs are finite; a program needn't handle non-finite values.
Results may differ from the reference program's by a relative error of at most 0.019.
Values may be sent and summed in bfloat16 or wider, within the bound.
A program may use at most 64 MiB of HBM per device.

```python
import math
import jax
import jax.numpy as jnp
from jax import lax

HD = 128
GROUP_CH = 16
FEAT = 7
FILT = 128
TOKENS = 2048
WIDTH = 512


def attention_pair(key):
    queries = jnp.clip(jax.random.normal(jax.random.fold_in(key, 101), (TOKENS, WIDTH), jnp.float32), -6.0, 6.0)
    keys_drawn = jnp.clip(jax.random.normal(jax.random.fold_in(key, 102), (TOKENS, WIDTH), jnp.float32), -6.0, 6.0)
    return (queries, keys_drawn)


def draw_q_att(key, part):
    return attention_pair(key)[0].astype(jnp.bfloat16)


def draw_k_att(key, part):
    return attention_pair(key)[1].astype(jnp.bfloat16)


def draw_v_att(key, part):
    channel = jnp.arange(WIDTH) // HD
    position = channel.astype(jnp.float32) / max(WIDTH // HD - 1, 1)
    base = jnp.clip(jax.random.normal(key, (TOKENS, WIDTH), jnp.float32), -3.4, 3.4)
    return (base * jnp.power(3.0, 0.5 * position)[None, :]).astype(jnp.bfloat16)


def shard_levels(key, shape, cuts, smallest, high):
    factor_of = 1.0
    for dim, shards_of in cuts:
        steps = jax.random.uniform(jax.random.fold_in(jax.random.fold_in(key, 6), dim), (shards_of,), jnp.float32, smallest / len(cuts), high / len(cuts))
        factor_of = factor_of * jnp.repeat(jnp.exp(steps), shape[dim] // shards_of).reshape((-1,) + (1,) * (len(shape) - 1 - dim))
    return factor_of


def noise(own_key, extent, deviation, most, split=(), kind=jnp.bfloat16):
    array = deviation * jax.random.normal(own_key, extent, jnp.float32)
    if split:
        array = array * shard_levels(own_key, extent, split, -0.22, 0.18)
    return jnp.clip(array, -most, most).astype(kind)


def setup_inputs(seed: int = 0) -> dict:
    seeds = jax.random.split(jax.random.key(seed), 10)
    q_att = draw_q_att(jax.random.fold_in(seeds[9], 71), 0)
    k_att = draw_k_att(jax.random.fold_in(seeds[9], 71), 0)
    v_att = draw_v_att(jax.random.fold_in(seeds[9], 71), 0)
    norm_gain = jnp.clip(1.0 + 0.15 * jax.random.normal(seeds[3], (WIDTH,), jnp.float32), 0.25, 1.75)
    hy_q = noise(seeds[4], (TOKENS, WIDTH), 1.0, 6.0, ((0, 8), (1, 4)))
    hy_k = noise(seeds[5], (TOKENS, WIDTH), 1.0, 6.0, ((0, 8), (1, 4)))
    feat_w = noise(seeds[6], (3, FEAT, WIDTH), FEAT ** -0.5, 2.0, ((2, 4),), jnp.float32)
    mr_filt = noise(seeds[7], (FILT, WIDTH // GROUP_CH), FILT ** -0.5, 0.5, ((1, 4),), jnp.float32)
    cotangent = noise(seeds[8], (TOKENS, WIDTH), 1.0, 6.0, ((0, 8), (1, 4)))
    return {"q_att": q_att, "k_att": k_att, "v_att": v_att, "norm_gain": norm_gain, "hy_q": hy_q, "hy_k": hy_k, "feat_w": feat_w, "mr_filt": mr_filt, "cotangent": cotangent}


NEGATIVE = -1e+30
EPSILON = 1e-06

def attention(queries, keys, values):
    total_rows, width = queries.shape
    heads = width // HD
    query_heads = queries.astype(jnp.float32).reshape(total_rows, heads, HD)
    key_heads = keys.astype(jnp.float32).reshape(total_rows, heads, HD)
    value_heads = values.astype(jnp.float32).reshape(total_rows, heads, HD)
    block = math.gcd(total_rows, 256)
    key_pos = jnp.arange(total_rows, dtype=jnp.int32)

    def one_block(begin):
        query_block = lax.dynamic_slice_in_dim(query_heads, begin.astype(jnp.int32), block, 0)
        scores = jnp.einsum('thd,phd->htp', query_block, key_heads) / math.sqrt(HD)
        query_pos = begin.astype(jnp.int32) + jnp.arange(block, dtype=jnp.int32)
        allowed = key_pos[None, :] <= query_pos[:, None]
        scores = jnp.where(allowed[None], scores, NEGATIVE)
        top = lax.optimization_barrier(jnp.max(scores, axis=-1, keepdims=True))
        probs = jnp.where(allowed[None], jnp.exp(scores - top), 0.0)
        totals = lax.optimization_barrier(jnp.sum(probs, axis=-1))
        weights = probs.astype(jnp.bfloat16).astype(jnp.float32)
        summed = jnp.einsum('htp,phd->thd', weights, value_heads)
        result = summed / jnp.transpose(totals)[:, :, None]
        return result.reshape(block, width).astype(jnp.bfloat16)
    starts = jnp.arange(total_rows // block, dtype=jnp.int32) * block
    return lax.map(one_block, starts).reshape(total_rows, width)

def causal_feature(stream, taps):
    width = taps.shape[0]
    count = stream.shape[0]
    padded = jnp.pad(stream.astype(jnp.float32), ((width - 1, 0), (0, 0)))
    total = jnp.zeros(stream.shape, jnp.float32)
    for lag in range(width):
        total = total + taps[lag] * padded[width - 1 - lag:width - 1 - lag + count]
    return total

def feature_back(grad, taps):
    width = taps.shape[0]
    count = grad.shape[0]
    padded = jnp.pad(grad.astype(jnp.float32), ((0, width - 1), (0, 0)))
    total = jnp.zeros(grad.shape, jnp.float32)
    for lag in range(width):
        total = total + taps[lag] * padded[lag:lag + count]
    return total

def long_conv(mixed, taps_ch):
    length = taps_ch.shape[0]
    count = mixed.shape[0]
    padded = jnp.pad(mixed, ((length - 1, 0), (0, 0)))

    def add_tap(lag, total):
        begin = (length - 1 - lag).astype(jnp.int32)
        return total + taps_ch[lag] * lax.dynamic_slice_in_dim(padded, begin, count, 0)
    return lax.fori_loop(0, length, add_tap, jnp.zeros(mixed.shape, jnp.float32))

def long_back(grad, taps_ch):
    length = taps_ch.shape[0]
    count = grad.shape[0]
    padded = jnp.pad(grad, ((0, length - 1), (0, 0)))

    def add_tap(lag, total):
        begin = lag.astype(jnp.int32)
        return total + taps_ch[lag] * lax.dynamic_slice_in_dim(padded, begin, count, 0)
    return lax.fori_loop(0, length, add_tap, jnp.zeros(grad.shape, jnp.float32))

def reference(q_att, k_att, v_att, norm_gain, hy_q, hy_k, feat_w, mr_filt, cotangent):
    attended = attention(q_att, k_att, v_att).astype(jnp.float32)
    mean_sq = lax.optimization_barrier(jnp.mean(attended * attended, axis=1, keepdims=True))
    value_stream = (attended * lax.rsqrt(mean_sq + EPSILON) * norm_gain).astype(jnp.bfloat16)
    q_feat = causal_feature(hy_q, feat_w[0]).astype(jnp.bfloat16).astype(jnp.float32)
    k_feat = causal_feature(hy_k, feat_w[1]).astype(jnp.bfloat16).astype(jnp.float32)
    v_feat = causal_feature(value_stream, feat_w[2]).astype(jnp.bfloat16).astype(jnp.float32)
    mixed = (k_feat * v_feat).astype(jnp.bfloat16).astype(jnp.float32)
    taps_ch = jnp.repeat(mr_filt, GROUP_CH, axis=1)
    signal = long_conv(mixed, taps_ch)
    output = (q_feat * signal).astype(jnp.bfloat16)
    grad_out = cotangent.astype(jnp.float32)
    d_signal = (grad_out * q_feat).astype(jnp.bfloat16).astype(jnp.float32)
    d_qf = (grad_out * signal).astype(jnp.bfloat16)
    d_mixed = long_back(d_signal, taps_ch)
    d_kf = (d_mixed * v_feat).astype(jnp.bfloat16)
    d_vf = (d_mixed * k_feat).astype(jnp.bfloat16)
    grad_q = feature_back(d_qf, feat_w[0]).astype(jnp.bfloat16)
    grad_k = feature_back(d_kf, feat_w[1]).astype(jnp.bfloat16)
    grad_v = feature_back(d_vf, feat_w[2]).astype(jnp.bfloat16)
    return (output, grad_q, grad_k, grad_v)
```

```python
import functools
import math

import jax
import jax.numpy as jnp
from jax import lax
from jax.experimental import pallas as pl
from jax.experimental.pallas import tpu as pltpu
from jax.sharding import PartitionSpec as P

HD = 128
GROUP_CH = 16
FEAT = 7
FILT = 128
NEGATIVE = -1e30
EPSILON = 1e-06
FAR = 144
NEAR = 16
MESH = pl.DeviceIdType.MESH
F32 = jnp.float32
BF16 = jnp.bfloat16


def taps_sum(ref, start, count, weights, step):
    total = weights[0:1] * ref[pl.ds(start, count), :]
    for lag in range(1, FEAT):
        total = total + weights[lag : lag + 1] * ref[pl.ds(start + step * lag, count), :]
    return total


def band_product(taps_ref, window_ref, groups, lane_group):
    wide = jnp.concatenate([window_ref[0:256, :], window_ref[128:384, :]], 1)
    short = jnp.concatenate([taps_ref[g * FILT : g * FILT + NEAR, :] for g in range(groups)], 0)
    last = jnp.dot(short, window_ref[256:512, :], preferred_element_type=F32)
    first = second = third = None
    for g in range(groups):
        both = jnp.dot(taps_ref[g * FILT : (g + 1) * FILT, :], wide, preferred_element_type=F32)
        end = last[g * NEAR : (g + 1) * NEAR]
        if g == 0:
            first, second, third = both[:, :128], both[:, 128:], end
        else:
            mine = lane_group == g
            first = jnp.where(mine, both[:, :128], first)
            second = jnp.where(mine, both[:, 128:], second)
            third = jnp.where(mine, end, third)
    return jnp.concatenate([first, second, third], 0)


def kernel(
    n,
    heads,
    width,
    q_ref,
    k_ref,
    v_ref,
    gain_ref,
    hyq_ref,
    hyk_ref,
    fw_ref,
    mr_ref,
    cot_ref,
    out_ref,
    gq_ref,
    gk_ref,
    gv_ref,
    kv,
    q_ext,
    aft_kv,
    hyk_ext,
    hyq_ext,
    cot_ext,
    squares,
    taps_f,
    taps_b,
    win_f,
    win_b,
    m_ref,
    l_ref,
    acc_ref,
    x32,
    y32,
    dq32,
    dk32,
    dv32,
    halo_send,
    halo_recv,
    kv_send,
    fwd_send,
    kv_recv,
    sib_send,
    sq_send,
    sq_recv,
):
    count = q_ref.shape[0]
    groups = mr_ref.shape[1]
    rows = FAR + count + NEAR
    chips = n // 2
    me = lax.axis_index("ctx")
    head = lax.axis_index("head")
    chip = me // 2
    core = lax.rem(me, 2)
    sibling = me + 1 - 2 * core

    barrier = pltpu.get_barrier_semaphore()

    def greet_ctx(d, c):
        pl.semaphore_signal(
            barrier, inc=1, device_id={"ctx": lax.rem(me + d, n)}, device_id_type=MESH
        )
        return c

    lax.fori_loop(1, n, greet_ctx, 0)
    for d in range(1, heads):
        pl.semaphore_signal(
            barrier, inc=1, device_id={"head": lax.rem(head + d, heads)}, device_id_type=MESH
        )
    kv[me, 0] = k_ref[...]
    kv[me, 1] = v_ref[...]
    q_ext[FAR : FAR + count, :] = q_ref[...]
    hyk_ext[FAR : FAR + count, :] = hyk_ref[...]
    hyq_ext[NEAR : NEAR + count, :] = hyq_ref[...]
    cot_ext[0:count, :] = cot_ref[...]

    def halo(index, src, dst, target):
        return pltpu.make_async_remote_copy(
            src_ref=src,
            dst_ref=dst,
            send_sem=halo_send.at[index],
            recv_sem=halo_recv.at[index],
            device_id={"ctx": target},
            device_id_type=MESH,
        )

    up = jnp.minimum(me + 1, n - 1)
    down = jnp.maximum(me - 1, 0)
    tail = pl.ds(count - FAR, FAR)
    onward = [
        halo(0, q_ref.at[tail, :], q_ext.at[pl.ds(0, FAR), :], up),
        halo(1, hyk_ref.at[tail, :], hyk_ext.at[pl.ds(0, FAR), :], up),
        halo(2, hyq_ref.at[pl.ds(count - NEAR, NEAR), :], hyq_ext.at[pl.ds(0, NEAR), :], up),
    ]
    near = pl.ds(0, NEAR)
    far = pl.ds(0, FAR)
    back = [
        halo(3, hyq_ref.at[far, :], hyq_ext.at[pl.ds(NEAR + count, FAR), :], down),
        halo(4, cot_ref.at[far, :], cot_ext.at[pl.ds(count, FAR), :], down),
        halo(5, q_ref.at[near, :], q_ext.at[pl.ds(FAR + count, NEAR), :], down),
        halo(6, hyk_ref.at[near, :], hyk_ext.at[pl.ds(FAR + count, NEAR), :], down),
        halo(7, k_ref.at[near, :], aft_kv.at[0], down),
        halo(8, v_ref.at[near, :], aft_kv.at[1], down),
    ]

    def kv_copy(slot, target, sem):
        return pltpu.make_async_remote_copy(
            src_ref=kv.at[slot],
            dst_ref=kv.at[slot],
            send_sem=sem,
            recv_sem=kv_recv.at[slot],
            device_id={"ctx": target},
            device_id_type=MESH,
        )

    pl.semaphore_wait(barrier, n + heads - 2)

    @pl.when(me < n - 1)
    def _():
        for copy in onward:
            copy.start()

    @pl.when(me > 0)
    def _():
        for copy in back:
            copy.start()

    def send_own(d, c):
        kv_copy(me, me + 2 * d, kv_send.at[d]).start()
        return c

    lax.fori_loop(1, chips - chip, send_own, 0)

    @pl.when(core == 0)
    def _():
        kv_copy(me, sibling, sib_send).start()

    @pl.when(me == 0)
    def _():
        q_ext[0:FAR, :] = jnp.zeros((FAR, HD), BF16)
        hyk_ext[0:FAR, :] = jnp.zeros((FAR, HD), BF16)
        hyq_ext[0:NEAR, :] = jnp.zeros((NEAR, HD), BF16)

    @pl.when(me == n - 1)
    def _():
        hyq_ext[NEAR + count : NEAR + count + FAR, :] = jnp.zeros((FAR, HD), BF16)
        cot_ext[count : count + FAR, :] = jnp.zeros((FAR, HD), BF16)
        q_ext[FAR + count :, :] = jnp.zeros((NEAR, HD), BF16)
        hyk_ext[FAR + count :, :] = jnp.zeros((NEAR, HD), BF16)
        aft_kv[...] = jnp.zeros(aft_kv.shape, BF16)

    tap = lax.broadcasted_iota(jnp.int32, (FILT, 2 * FILT), 0)
    col = lax.broadcasted_iota(jnp.int32, (FILT, 2 * FILT), 1)
    taps16 = mr_ref[...].astype(BF16)
    over_rows = (((0,), (0,)), ((), ()))
    for out_taps, place in ((taps_b, tap == col), (taps_f, tap == FILT - col)):
        line = lax.dot_general(
            taps16, place.astype(F32).astype(BF16), over_rows, preferred_element_type=F32
        )
        for g in range(groups):
            spread = jnp.broadcast_to(line[g : g + 1, :], (FILT, 2 * FILT))
            moved = pltpu.roll(spread, 0, 1, stride=1, stride_axis=0)
            out_taps[g * FILT : (g + 1) * FILT, :] = moved.astype(BF16)

    scale = math.log2(math.e) / math.sqrt(HD)
    over_last = (((1,), (1,)), ((), ()))

    def attend(start, size, keys, values, key_base, masked):
        part = pl.ds(start, size)
        scores = lax.dot_general(q_ext[part, :], keys, over_last, preferred_element_type=F32)
        if masked:
            row = lax.broadcasted_iota(jnp.int32, scores.shape, 0) + (start - FAR)
            at = lax.broadcasted_iota(jnp.int32, scores.shape, 1) + key_base
            scores = jnp.where(at <= row, scores, NEGATIVE)
        old = m_ref[part, :]
        new = jnp.maximum(old, jnp.max(scores, axis=1, keepdims=True))
        m_ref[part, :] = new
        factor = jnp.exp2((old - new) * scale)
        probs = jnp.exp2((scores - new[:, 0:1]) * scale)
        if probs.shape[1] == 2 * HD:
            sums = probs[:, :HD] + probs[:, HD:]
        else:
            lane0 = lax.broadcasted_iota(jnp.int32, (size, HD), 1) == 0
            sums = jnp.where(lane0, jnp.sum(probs, axis=1, keepdims=True), 0.0)
        l_ref[part, :] = l_ref[part, :] * factor + sums
        acc_ref[part, :] = acc_ref[part, :] * factor + jnp.dot(
            probs.astype(BF16), values, preferred_element_type=F32
        )

    m_ref[...] = jnp.full(m_ref.shape, NEGATIVE, F32)
    l_ref[...] = jnp.zeros(l_ref.shape, F32)
    acc_ref[...] = jnp.zeros(acc_ref.shape, F32)

    @pl.when(me > 0)
    def _():
        for copy in onward:
            copy.wait_recv()

    @pl.when(me < n - 1)
    def _():
        for copy in back:
            copy.wait_recv()

    attend(0, rows, kv[me, 0], kv[me, 1], 0, True)
    attend(FAR + count, NEAR, aft_kv[0], aft_kv[1], count, True)

    lane_group = lax.broadcasted_iota(jnp.int32, (1, HD), 1) // GROUP_CH
    ext = 384 + NEAR
    x32[...] = hyq_ext[...].astype(F32)
    qf = taps_sum(x32, NEAR, ext, fw_ref[0], -1).astype(BF16).astype(F32)
    d_signal = (cot_ext[...].astype(F32) * qf).astype(BF16)
    win_b[0:ext, :] = d_signal
    win_b[ext:, :] = jnp.zeros((512 - ext, HD), BF16)
    win_f[ext:, :] = jnp.zeros((512 - ext, HD), BF16)
    y32[...] = hyk_ext[...].astype(F32)
    kf = taps_sum(y32, NEAR, ext, fw_ref[1], -1).astype(BF16).astype(F32)
    near_rows = count + NEAR
    d_mixed = band_product(taps_b, win_b, groups, lane_group)
    dv32[...] = (d_mixed * kf[FILT : FILT + near_rows]).astype(BF16).astype(F32)
    gv_ref[...] = taps_sum(dv32, 0, count, fw_ref[2], 1).astype(BF16)
    dk32[...] = d_mixed

    @pl.when(core == 1)
    def _():
        kv_copy(sibling, sibling, sib_send).wait_recv()
        attend(0, rows, kv[sibling, 0], kv[sibling, 1], -count, True)

    def remote(d, c):
        same = me - 2 * d
        other = sibling - 2 * d
        kv_copy(same, sibling, fwd_send.at[d]).wait_recv()
        kv_copy(same, sibling, fwd_send.at[d]).start()
        attend(0, rows, kv[same, 0], kv[same, 1], (same - me) * count, True)
        kv_copy(other, sibling, fwd_send.at[d]).wait_recv()
        attend(0, rows, kv[other, 0], kv[other, 1], (other - me) * count, True)
        return c

    lax.fori_loop(1, chip + 1, remote, 0)

    total = jnp.sum(l_ref[...], axis=1, keepdims=True)
    attended = (acc_ref[...] / total).astype(BF16).astype(F32)
    squares[head] = jnp.zeros((8, 512), F32)
    squares[head, :, 0:rows] = lax.dot_general(
        jnp.ones((8, HD), F32),
        attended * attended,
        over_last,
        precision=lax.Precision.HIGHEST,
        preferred_element_type=F32,
    )

    def sq_copy(d):
        return pltpu.make_async_remote_copy(
            src_ref=squares.at[head],
            dst_ref=squares.at[head],
            send_sem=sq_send.at[d],
            recv_sem=sq_recv.at[d],
            device_id={"head": lax.rem(head + d, heads)},
            device_id_type=MESH,
        )

    for d in range(1, heads):
        sq_copy(d).start()
    for d in range(1, heads):
        sq_copy(d).wait_recv()
    whole = squares[0]
    for other in range(1, heads):
        whole = whole + squares[other]
    mean_sq = lax.dot_general(
        whole,
        jnp.full((8, HD), 1.0 / (8 * width), F32),
        over_rows,
        precision=lax.Precision.HIGHEST,
        preferred_element_type=F32,
    )[0:rows]
    value = (attended * lax.rsqrt(mean_sq + EPSILON) * gain_ref[...]).astype(BF16).astype(F32)
    place = lax.broadcasted_iota(jnp.int32, value.shape, 0) + (me * count - FAR)
    x32[...] = jnp.where((place >= 0) & (place < n * count), value, 0.0)
    vf = taps_sum(x32, NEAR, ext, fw_ref[2], -1).astype(BF16).astype(F32)
    win_f[0:ext, :] = (kf * vf).astype(BF16)
    signal = band_product(taps_f, win_f, groups, lane_group)
    out_ref[...] = (qf[0:count] * signal[0:count]).astype(BF16)
    dq32[...] = (cot_ext[0:near_rows, :].astype(F32) * signal).astype(BF16).astype(F32)
    gq_ref[...] = taps_sum(dq32, 0, count, fw_ref[0], 1).astype(BF16)
    dk32[...] = (dk32[...] * vf[FILT : FILT + near_rows]).astype(BF16).astype(F32)
    gk_ref[...] = taps_sum(dk32, 0, count, fw_ref[1], 1).astype(BF16)

    @pl.when(me < n - 1)
    def _():
        for copy in onward:
            copy.wait_send()

    @pl.when(me > 0)
    def _():
        for copy in back:
            copy.wait_send()

    @pl.when(core == 0)
    def _():
        kv_copy(me, sibling, sib_send).wait_send()

    def sent_own(d, c):
        kv_copy(me, me + 2 * d, kv_send.at[d]).wait_send()
        return c

    lax.fori_loop(1, chips - chip, sent_own, 0)

    def sent_on(d, c):
        kv_copy(me - 2 * d, sibling, fwd_send.at[d]).wait_send()
        return c

    lax.fori_loop(1, chip + 1, sent_on, 0)
    for d in range(1, heads):
        sq_copy(d).wait_send()


def per_device(q_att, k_att, v_att, norm_gain, hy_q, hy_k, feat_w, mr_filt, cotangent):
    count, channels = q_att.shape
    n = lax.axis_size("ctx")
    heads = lax.axis_size("head")
    groups = mr_filt.shape[1]
    rows = FAR + count + NEAR
    block = jax.ShapeDtypeStruct((count, channels), BF16)
    vmem = pl.BlockSpec(memory_space=pltpu.VMEM)
    dma = pltpu.SemaphoreType.DMA
    near_rows = count + NEAR
    return pl.pallas_call(
        functools.partial(kernel, n, heads, channels * heads),
        out_shape=(block,) * 4,
        in_specs=[vmem] * 9,
        out_specs=(vmem,) * 4,
        scratch_shapes=[
            pltpu.VMEM((n, 2, count, HD), BF16),
            pltpu.VMEM((rows, HD), BF16),
            pltpu.VMEM((2, NEAR, HD), BF16),
            pltpu.VMEM((rows, HD), BF16),
            pltpu.VMEM((rows, HD), BF16),
            pltpu.VMEM((count + FAR, HD), BF16),
            pltpu.VMEM((heads, 8, 512), F32),
            pltpu.VMEM((groups * FILT, 2 * FILT), BF16),
            pltpu.VMEM((groups * FILT, 2 * FILT), BF16),
            pltpu.VMEM((512, HD), BF16),
            pltpu.VMEM((512, HD), BF16),
            pltpu.VMEM((rows, HD), F32),
            pltpu.VMEM((rows, HD), F32),
            pltpu.VMEM((rows, HD), F32),
            pltpu.VMEM((rows, HD), F32),
            pltpu.VMEM((rows, HD), F32),
            pltpu.VMEM((near_rows, HD), F32),
            pltpu.VMEM((near_rows, HD), F32),
            pltpu.VMEM((near_rows, HD), F32),
            dma((9,)),
            dma((9,)),
            dma((n // 2,)),
            dma((n // 2,)),
            dma((n,)),
            dma,
            dma((heads,)),
            dma((heads,)),
        ],
        compiler_params=pltpu.CompilerParams(
            collective_id=0, has_side_effects=True, vmem_limit_bytes=40 * 1024 * 1024
        ),
    )(q_att, k_att, v_att, norm_gain.reshape(1, channels), hy_q, hy_k, feat_w, mr_filt, cotangent)


def solution(mesh):
    placed = (
        P("ctx", "head"),
        P("ctx", "head"),
        P("ctx", "head"),
        P("head"),
        P("ctx", "head"),
        P("ctx", "head"),
        P(None, None, "head"),
        P(None, "head"),
        P("ctx", "head"),
    )
    return jax.shard_map(
        per_device,
        mesh=mesh,
        in_specs=placed,
        out_specs=(P("ctx", "head"),) * 4,
        check_vma=False,
    )
```

```python
import functools
import math

import jax
import jax.numpy as jnp
from jax import lax
from jax.experimental import pallas as pl
from jax.experimental.pallas import tpu as pltpu
from jax.sharding import PartitionSpec as P

HD = 128
GROUP_CH = 16
FEAT = 7
FILT = 128
NEGATIVE = -1e30
EPSILON = 1e-06
FAR = 144
NEAR = 16
MESH = pl.DeviceIdType.MESH
F32 = jnp.float32
BF16 = jnp.bfloat16


def taps_sum(ref, start, count, weights, step):
    total = weights[0:1] * ref[pl.ds(start, count), :]
    for lag in range(1, FEAT):
        total = total + weights[lag : lag + 1] * ref[pl.ds(start + step * lag, count), :]
    return total


def band_product(taps_ref, window_ref, groups, lane_group):
    wide = jnp.concatenate([window_ref[0:256, :], window_ref[128:384, :]], 1)
    short = jnp.concatenate([taps_ref[g * FILT : g * FILT + NEAR, :] for g in range(groups)], 0)
    last = jnp.dot(short, window_ref[256:512, :], preferred_element_type=F32)
    first = second = third = None
    for g in range(groups):
        both = jnp.dot(taps_ref[g * FILT : (g + 1) * FILT, :], wide, preferred_element_type=F32)
        end = last[g * NEAR : (g + 1) * NEAR]
        if g == 0:
            first, second, third = both[:, :128], both[:, 128:], end
        else:
            mine = lane_group == g
            first = jnp.where(mine, both[:, :128], first)
            second = jnp.where(mine, both[:, 128:], second)
            third = jnp.where(mine, end, third)
    return jnp.concatenate([first, second, third], 0)


def kernel(
    n,
    heads,
    width,
    q_ref,
    k_ref,
    v_ref,
    gain_hbm,
    hyq_ref,
    hyk_ref,
    fw_hbm,
    mr_hbm,
    cot_ref,
    packed_ref,
    kv,
    q_ext,
    aft_kv,
    hyk_ext,
    hyq_ext,
    cot_ext,
    squares,
    taps_f,
    taps_b,
    win_f,
    win_b,
    m_ref,
    l_ref,
    acc_ref,
    x32,
    y32,
    dq32,
    dk32,
    dv32,
    gain_ref,
    fw_ref,
    mr_ref,
    stage,
    local_sem,
    out_sem,
    halo_send,
    halo_recv,
    kv_send,
    fwd_send,
    relay_send,
    kv_recv,
    sib_send,
    sq_send,
    sq_recv,
):
    count = q_ref.shape[0]
    groups = mr_ref.shape[0]
    rows = FAR + count + NEAR
    chips = n // 2
    me = lax.axis_index("ctx")
    head = lax.axis_index("head")
    chip = me // 2
    core = lax.rem(me, 2)
    sibling = me + 1 - 2 * core

    moves = (
        (k_ref, kv.at[0, me]),
        (v_ref, kv.at[1, me]),
        (mr_hbm, mr_ref),
        (q_ref, q_ext.at[pl.ds(FAR, count), :]),
        (hyq_ref, hyq_ext.at[pl.ds(NEAR, count), :]),
        (cot_ref, cot_ext.at[pl.ds(0, count), :]),
        (fw_hbm, fw_ref),
        (hyk_ref, hyk_ext.at[pl.ds(FAR, count), :]),
        (gain_hbm, gain_ref),
    )
    loads = [
        pltpu.make_async_copy(src, dst, local_sem.at[index])
        for index, (src, dst) in enumerate(moves)
    ]
    for load in loads:
        load.start()

    barrier = pltpu.get_barrier_semaphore()

    def greet_ctx(d, c):
        pl.semaphore_signal(
            barrier, inc=1, device_id={"ctx": lax.rem(me + d, n)}, device_id_type=MESH
        )
        return c

    lax.fori_loop(1, n, greet_ctx, 0)
    for d in range(1, heads):
        pl.semaphore_signal(
            barrier, inc=1, device_id={"head": lax.rem(head + d, heads)}, device_id_type=MESH
        )

    def halo(index, src, dst, target):
        return pltpu.make_async_remote_copy(
            src_ref=src,
            dst_ref=dst,
            send_sem=halo_send.at[index],
            recv_sem=halo_recv.at[index],
            device_id={"ctx": target},
            device_id_type=MESH,
        )

    up = jnp.minimum(me + 1, n - 1)
    down = jnp.maximum(me - 1, 0)
    tail = pl.ds(count - FAR, FAR)
    onward = [
        halo(0, q_ref.at[tail, :], q_ext.at[pl.ds(0, FAR), :], up),
        halo(1, hyk_ref.at[tail, :], hyk_ext.at[pl.ds(0, FAR), :], up),
        halo(2, hyq_ref.at[pl.ds(count - NEAR, NEAR), :], hyq_ext.at[pl.ds(0, NEAR), :], up),
    ]
    near = pl.ds(0, NEAR)
    far = pl.ds(0, FAR)
    back = [
        halo(3, hyq_ref.at[far, :], hyq_ext.at[pl.ds(NEAR + count, FAR), :], down),
        halo(4, cot_ref.at[far, :], cot_ext.at[pl.ds(count, FAR), :], down),
        halo(5, q_ref.at[near, :], q_ext.at[pl.ds(FAR + count, NEAR), :], down),
        halo(6, hyk_ref.at[near, :], hyk_ext.at[pl.ds(FAR + count, NEAR), :], down),
        halo(7, k_ref.at[near, :], aft_kv.at[0], down),
        halo(8, v_ref.at[near, :], aft_kv.at[1], down),
    ]

    def kv_copy(half, slot, target, sem):
        return pltpu.make_async_remote_copy(
            src_ref=kv.at[half, slot],
            dst_ref=kv.at[half, slot],
            send_sem=sem,
            recv_sem=kv_recv.at[half, slot],
            device_id={"ctx": target},
            device_id_type=MESH,
        )

    square = chips == 4

    def each_own(act):
        def one(d, c):
            for half in range(2):
                act(kv_copy(half, me, me + 2 * d, kv_send.at[half, d]))
            return c

        if square:

            @pl.when(chip != 1)
            def _():
                lax.fori_loop(1, jnp.minimum(chips - chip, 3), one, 0)

            @pl.when(chip == 1)
            def _():
                one(2, 0)
        else:
            lax.fori_loop(1, chips - chip, one, 0)

    def each_relay(half, earlier, act):
        if not square:
            return

        @pl.when((chip == 1 + half) & (earlier == 0))
        def _():
            act(kv_copy(half, core, 6 + core, relay_send.at[half]))

        @pl.when((chip == 3) & (earlier == 1))
        def _():
            act(kv_copy(half, 2 + core, 4 + core, relay_send.at[half]))

    def source(step):
        if square:
            return lax.rem(step + jnp.where(chip == 3, 1, 0), jnp.maximum(chip, 1))
        return chip - 1 - step

    pl.semaphore_wait(barrier, n + heads - 2)
    loads[0].wait()
    loads[1].wait()

    @pl.when(me < n - 1)
    def _():
        for copy in onward:
            copy.start()

    @pl.when(me > 0)
    def _():
        for copy in back:
            copy.start()

    each_own(lambda copy: copy.start())

    @pl.when(core == 0)
    def _():
        for half in range(2):
            kv_copy(half, me, sibling, sib_send.at[half]).start()

    @pl.when(me == 0)
    def _():
        q_ext[0:FAR, :] = jnp.zeros((FAR, HD), BF16)
        hyk_ext[0:FAR, :] = jnp.zeros((FAR, HD), BF16)
        hyq_ext[0:NEAR, :] = jnp.zeros((NEAR, HD), BF16)

    @pl.when(me == n - 1)
    def _():
        hyq_ext[NEAR + count : NEAR + count + FAR, :] = jnp.zeros((FAR, HD), BF16)
        cot_ext[count : count + FAR, :] = jnp.zeros((FAR, HD), BF16)
        q_ext[FAR + count :, :] = jnp.zeros((NEAR, HD), BF16)
        hyk_ext[FAR + count :, :] = jnp.zeros((NEAR, HD), BF16)
        aft_kv[...] = jnp.zeros(aft_kv.shape, BF16)

    loads[2].wait()

    tap = lax.broadcasted_iota(jnp.int32, (FILT, 2 * FILT), 0)
    col = lax.broadcasted_iota(jnp.int32, (FILT, 2 * FILT), 1)
    taps16 = mr_ref[...].astype(BF16)
    for out_taps, place in ((taps_b, tap == col), (taps_f, tap == FILT - col)):
        line = jnp.dot(taps16, place.astype(F32).astype(BF16), preferred_element_type=F32)
        for g in range(groups):
            spread = jnp.broadcast_to(line[g : g + 1, :], (FILT, 2 * FILT))
            moved = pltpu.roll(spread, 0, 1, stride=1, stride_axis=0)
            out_taps[g * FILT : (g + 1) * FILT, :] = moved.astype(BF16)

    scale = math.log2(math.e) / math.sqrt(HD)
    over_last = (((1,), (1,)), ((), ()))

    def attend(start, size, keys, values, key_base, masked):
        part = pl.ds(start, size)
        scores = lax.dot_general(q_ext[part, :], keys, over_last, preferred_element_type=F32)
        if masked:
            row = lax.broadcasted_iota(jnp.int32, scores.shape, 0) + (start - FAR)
            at = lax.broadcasted_iota(jnp.int32, scores.shape, 1) + key_base
            scores = jnp.where(at <= row, scores, NEGATIVE)
        old = m_ref[part, :]
        new = jnp.maximum(old, jnp.max(scores, axis=1, keepdims=True))
        m_ref[part, :] = new
        factor = jnp.exp2((old - new) * scale)
        probs = jnp.exp2((scores - new[:, 0:1]) * scale)
        if probs.shape[1] >= HD:
            sums = probs[:, :HD]
            for begin in range(HD, probs.shape[1], HD):
                sums = sums + probs[:, begin : begin + HD]
        else:
            lane0 = lax.broadcasted_iota(jnp.int32, (size, HD), 1) == 0
            sums = jnp.where(lane0, jnp.sum(probs, axis=1, keepdims=True), 0.0)
        l_ref[part, :] = l_ref[part, :] * factor + sums
        acc_ref[part, :] = acc_ref[part, :] * factor + jnp.dot(
            probs.astype(BF16), values, preferred_element_type=F32
        )

    m_ref[...] = jnp.full(m_ref.shape, NEGATIVE, F32)
    l_ref[...] = jnp.zeros(l_ref.shape, F32)
    acc_ref[...] = jnp.zeros(acc_ref.shape, F32)

    @pl.when(me > 0)
    def _():
        for copy in onward:
            copy.wait_recv()

    @pl.when(me < n - 1)
    def _():
        for copy in back:
            copy.wait_recv()

    for load in loads[3:]:
        load.wait()
    attend(0, rows, kv[0, me], kv[1, me], 0, True)
    attend(FAR + count, NEAR, aft_kv[0], aft_kv[1], count, True)

    lane_group = lax.broadcasted_iota(jnp.int32, (1, HD), 1) // GROUP_CH
    ext = 384 + NEAR
    x32[...] = hyq_ext[...].astype(F32)
    qf = taps_sum(x32, NEAR, ext, fw_ref[0], -1).astype(BF16).astype(F32)
    d_signal = (cot_ext[...].astype(F32) * qf).astype(BF16)
    win_b[0:ext, :] = d_signal
    win_b[ext:, :] = jnp.zeros((512 - ext, HD), BF16)
    win_f[ext:, :] = jnp.zeros((512 - ext, HD), BF16)
    y32[...] = hyk_ext[...].astype(F32)
    kf = taps_sum(y32, NEAR, ext, fw_ref[1], -1).astype(BF16).astype(F32)
    near_rows = count + NEAR
    d_mixed = band_product(taps_b, win_b, groups, lane_group)
    dv32[...] = (d_mixed * kf[FILT : FILT + near_rows]).astype(BF16).astype(F32)
    stage[3] = taps_sum(dv32, 0, count, fw_ref[2], 1).astype(BF16)
    stores = [
        pltpu.make_async_copy(stage.at[i], packed_ref.at[i], out_sem.at[i]) for i in range(4)
    ]
    stores[3].start()
    dk32[...] = d_mixed

    @pl.when(core == 1)
    def _():
        for half in range(2):
            kv_copy(half, sibling, sibling, sib_send.at[half]).wait_recv()
        attend(0, rows, kv[0, sibling], kv[1, sibling], -count, True)

    def bring(step):
        earlier = source(step)
        slot = 2 * earlier + core
        for half in range(2):
            kv_copy(half, slot, sibling, fwd_send.at[half, earlier]).wait_recv()
            each_relay(half, earlier, lambda copy: copy.start())
            kv_copy(half, slot, sibling, fwd_send.at[half, earlier]).start()

    def use(step):
        earlier = source(step)
        slot = 2 * earlier + 1 - core
        for half in range(2):
            kv_copy(half, slot, sibling, fwd_send.at[half, earlier]).wait_recv()
        keys = kv[0, pl.ds(2 * earlier, 2)].reshape(2 * count, HD)
        values = kv[1, pl.ds(2 * earlier, 2)].reshape(2 * count, HD)
        attend(0, rows, keys, values, (2 * earlier - me) * count, True)

    @pl.when(chip > 0)
    def _():
        bring(0)

    def remote(step, c):
        bring(step)
        use(step - 1)
        return c

    lax.fori_loop(1, chip, remote, 0)

    @pl.when(chip > 0)
    def _():
        use(chip - 1)

    total = jnp.sum(l_ref[...], axis=1, keepdims=True)
    attended = (acc_ref[...] / total).astype(BF16).astype(F32)
    squares[head] = jnp.zeros((8, 512), F32)
    squares[head, :, 0:rows] = lax.dot_general(
        jnp.ones((8, HD), F32),
        attended * attended,
        over_last,
        precision=lax.Precision.HIGHEST,
        preferred_element_type=F32,
    )

    def sq_copy(d):
        return pltpu.make_async_remote_copy(
            src_ref=squares.at[head],
            dst_ref=squares.at[head],
            send_sem=sq_send.at[d],
            recv_sem=sq_recv.at[d],
            device_id={"head": lax.rem(head + d, heads)},
            device_id_type=MESH,
        )

    for d in range(1, heads):
        sq_copy(d).start()
    for d in range(1, heads):
        sq_copy(d).wait_recv()
    whole = squares[0]
    for other in range(1, heads):
        whole = whole + squares[other]
    mean_sq = lax.dot_general(
        whole,
        jnp.full((8, HD), 1.0 / (8 * width), F32),
        (((0,), (0,)), ((), ())),
        precision=lax.Precision.HIGHEST,
        preferred_element_type=F32,
    )[0:rows]
    value = (attended * lax.rsqrt(mean_sq + EPSILON) * gain_ref[...]).astype(BF16).astype(F32)
    place = lax.broadcasted_iota(jnp.int32, value.shape, 0) + (me * count - FAR)
    x32[...] = jnp.where((place >= 0) & (place < n * count), value, 0.0)
    vf = taps_sum(x32, NEAR, ext, fw_ref[2], -1).astype(BF16).astype(F32)
    win_f[0:ext, :] = (kf * vf).astype(BF16)
    signal = band_product(taps_f, win_f, groups, lane_group)
    stage[0] = (qf[0:count] * signal[0:count]).astype(BF16)
    stores[0].start()
    dq32[...] = (cot_ext[0:near_rows, :].astype(F32) * signal).astype(BF16).astype(F32)
    stage[1] = taps_sum(dq32, 0, count, fw_ref[0], 1).astype(BF16)
    stores[1].start()
    dk32[...] = (dk32[...] * vf[FILT : FILT + near_rows]).astype(BF16).astype(F32)
    stage[2] = taps_sum(dk32, 0, count, fw_ref[1], 1).astype(BF16)
    stores[2].start()

    @pl.when(me < n - 1)
    def _():
        for copy in onward:
            copy.wait_send()

    @pl.when(me > 0)
    def _():
        for copy in back:
            copy.wait_send()

    @pl.when(core == 0)
    def _():
        for half in range(2):
            kv_copy(half, me, sibling, sib_send.at[half]).wait_send()

    each_own(lambda copy: copy.wait_send())

    def sent_on(earlier, c):
        for half in range(2):
            kv_copy(half, 2 * earlier + core, sibling, fwd_send.at[half, earlier]).wait_send()
            each_relay(half, earlier, lambda copy: copy.wait_send())
        return c

    lax.fori_loop(0, chip, sent_on, 0)
    for d in range(1, heads):
        sq_copy(d).wait_send()
    for store in stores:
        store.wait()


def unpack(packed_ref, out_ref, gq_ref, gk_ref, gv_ref, stage, in_sems, sems):
    loads = [
        pltpu.make_async_copy(packed_ref.at[i], stage.at[i], in_sems.at[i]) for i in range(4)
    ]
    copies = [
        pltpu.make_async_copy(stage.at[i], dst, sems.at[i])
        for i, dst in enumerate((out_ref, gq_ref, gk_ref, gv_ref))
    ]
    for load in loads:
        load.start()
    for load, copy in zip(loads, copies):
        load.wait()
        copy.start()
    for copy in copies:
        copy.wait()


def per_device(q_att, k_att, v_att, norm_gain, hy_q, hy_k, feat_w, mr_filt, cotangent):
    count, channels = q_att.shape
    n = lax.axis_size("ctx")
    heads = lax.axis_size("head")
    groups = mr_filt.shape[1]
    depth = feat_w.shape[0]
    rows = FAR + count + NEAR
    block = jax.ShapeDtypeStruct((count, channels), BF16)
    dma = pltpu.SemaphoreType.DMA
    near_rows = count + NEAR
    hbm = pl.BlockSpec(memory_space=pltpu.HBM)
    packed = pl.pallas_call(
        functools.partial(kernel, n, heads, channels * heads),
        out_shape=jax.ShapeDtypeStruct((4, count, channels), BF16),
        in_specs=[hbm] * 9,
        out_specs=hbm,
        scratch_shapes=[
            pltpu.VMEM((2, n, count, HD), BF16),
            pltpu.VMEM((rows, HD), BF16),
            pltpu.VMEM((2, NEAR, HD), BF16),
            pltpu.VMEM((rows, HD), BF16),
            pltpu.VMEM((rows, HD), BF16),
            pltpu.VMEM((count + FAR, HD), BF16),
            pltpu.VMEM((heads, 8, 512), F32),
            pltpu.VMEM((groups * FILT, 2 * FILT), BF16),
            pltpu.VMEM((groups * FILT, 2 * FILT), BF16),
            pltpu.VMEM((512, HD), BF16),
            pltpu.VMEM((512, HD), BF16),
            pltpu.VMEM((rows, HD), F32),
            pltpu.VMEM((rows, HD), F32),
            pltpu.VMEM((rows, HD), F32),
            pltpu.VMEM((rows, HD), F32),
            pltpu.VMEM((rows, HD), F32),
            pltpu.VMEM((near_rows, HD), F32),
            pltpu.VMEM((near_rows, HD), F32),
            pltpu.VMEM((near_rows, HD), F32),
            pltpu.VMEM((1, HD), F32),
            pltpu.VMEM((depth, FEAT, HD), F32),
            pltpu.VMEM((groups, FILT), F32),
            pltpu.VMEM((4, count, HD), BF16),
            dma((9,)),
            dma((4,)),
            dma((9,)),
            dma((9,)),
            dma((2, n // 2)),
            dma((2, n // 2)),
            dma((2,)),
            dma((2, n)),
            dma((2,)),
            dma((heads,)),
            dma((heads,)),
        ],
        compiler_params=pltpu.CompilerParams(
            collective_id=0, has_side_effects=True, vmem_limit_bytes=63 * 1024 * 1024
        ),
    )(q_att, k_att, v_att, norm_gain.reshape(1, channels), hy_q, hy_k, feat_w, mr_filt.T, cotangent)
    return pl.pallas_call(
        unpack,
        out_shape=(block,) * 4,
        in_specs=[hbm],
        out_specs=(hbm,) * 4,
        scratch_shapes=[pltpu.VMEM((4, count, channels), BF16), dma((4,)), dma((4,))],
        compiler_params=pltpu.CompilerParams(vmem_limit_bytes=63 * 1024 * 1024),
    )(packed)


def solution(mesh):
    placed = (
        P("ctx", "head"),
        P("ctx", "head"),
        P("ctx", "head"),
        P("head"),
        P("ctx", "head"),
        P("ctx", "head"),
        P(None, None, "head"),
        P(None, "head"),
        P("ctx", "head"),
    )
    return jax.shard_map(
        per_device,
        mesh=mesh,
        in_specs=placed,
        out_specs=(P("ctx", "head"),) * 4,
        check_vma=False,
    )
```

```python
import functools
import math

import jax
import jax.numpy as jnp
from jax import lax
from jax.experimental import pallas as pl
from jax.experimental.pallas import tpu as pltpu
from jax.sharding import PartitionSpec as P

HD = 128
GROUP_CH = 16
FEAT = 7
FILT = 128
NEGATIVE = -1e30
EPSILON = 1e-06
FAR = 144
NEAR = 16
MESH = pl.DeviceIdType.MESH
F32 = jnp.float32
BF16 = jnp.bfloat16


def taps_sum(ref, start, count, weights, step):
    total = weights[0:1] * ref[pl.ds(start, count), :]
    for lag in range(1, FEAT):
        total = total + weights[lag : lag + 1] * ref[pl.ds(start + step * lag, count), :]
    return total


def band_product(taps_ref, window_ref, groups, lane_group):
    wide = jnp.concatenate([window_ref[0:256, :], window_ref[128:384, :]], 1)
    short = jnp.concatenate([taps_ref[g * FILT : g * FILT + NEAR, :] for g in range(groups)], 0)
    last = jnp.dot(short, window_ref[256:512, :], preferred_element_type=F32)
    first = second = third = None
    for g in range(groups):
        both = jnp.dot(taps_ref[g * FILT : (g + 1) * FILT, :], wide, preferred_element_type=F32)
        end = last[g * NEAR : (g + 1) * NEAR]
        if g == 0:
            first, second, third = both[:, :128], both[:, 128:], end
        else:
            mine = lane_group == g
            first = jnp.where(mine, both[:, :128], first)
            second = jnp.where(mine, both[:, 128:], second)
            third = jnp.where(mine, end, third)
    return jnp.concatenate([first, second, third], 0)


def kernel(
    n,
    heads,
    width,
    q_ref,
    k_ref,
    v_ref,
    gain_hbm,
    hyq_ref,
    hyk_ref,
    fw_hbm,
    mr_hbm,
    cot_ref,
    packed_ref,
    kv,
    q_ext,
    aft_kv,
    hyk_ext,
    hyq_ext,
    cot_ext,
    squares,
    taps_f,
    taps_b,
    win_f,
    win_b,
    m_ref,
    l_ref,
    acc_ref,
    x32,
    y32,
    dq32,
    dk32,
    dv32,
    gain_ref,
    fw_ref,
    mr_ref,
    stage,
    local_sem,
    out_sem,
    halo_send,
    halo_recv,
    kv_send,
    fwd_send,
    relay_send,
    kv_recv,
    sib_send,
    sq_send,
    sq_recv,
):
    count = q_ref.shape[0]
    groups = mr_ref.shape[0]
    rows = FAR + count + NEAR
    chips = n // 2
    me = lax.axis_index("ctx")
    head = lax.axis_index("head")
    chip = me // 2
    core = lax.rem(me, 2)
    sibling = me + 1 - 2 * core

    moves = (
        (k_ref, kv.at[0, me]),
        (v_ref, kv.at[1, me]),
        (mr_hbm, mr_ref),
        (q_ref, q_ext.at[pl.ds(FAR, count), :]),
        (hyq_ref, hyq_ext.at[pl.ds(NEAR, count), :]),
        (cot_ref, cot_ext.at[pl.ds(0, count), :]),
        (fw_hbm, fw_ref),
        (hyk_ref, hyk_ext.at[pl.ds(FAR, count), :]),
        (gain_hbm, gain_ref),
    )
    loads = [
        pltpu.make_async_copy(src, dst, local_sem.at[index])
        for index, (src, dst) in enumerate(moves)
    ]
    for load in loads:
        load.start()

    barrier = pltpu.get_barrier_semaphore()

    def greet_ctx(d, c):
        pl.semaphore_signal(
            barrier, inc=1, device_id={"ctx": lax.rem(me + d, n)}, device_id_type=MESH
        )
        return c

    lax.fori_loop(1, n, greet_ctx, 0)
    for d in range(1, heads):
        pl.semaphore_signal(
            barrier, inc=1, device_id={"head": lax.rem(head + d, heads)}, device_id_type=MESH
        )

    def halo(index, src, dst, target):
        return pltpu.make_async_remote_copy(
            src_ref=src,
            dst_ref=dst,
            send_sem=halo_send.at[index],
            recv_sem=halo_recv.at[index],
            device_id={"ctx": target},
            device_id_type=MESH,
        )

    up = jnp.minimum(me + 1, n - 1)
    down = jnp.maximum(me - 1, 0)
    tail = pl.ds(count - FAR, FAR)
    onward = [
        halo(0, q_ref.at[tail, :], q_ext.at[pl.ds(0, FAR), :], up),
        halo(1, hyk_ref.at[tail, :], hyk_ext.at[pl.ds(0, FAR), :], up),
        halo(2, hyq_ref.at[pl.ds(count - NEAR, NEAR), :], hyq_ext.at[pl.ds(0, NEAR), :], up),
    ]
    near = pl.ds(0, NEAR)
    far = pl.ds(0, FAR)
    back = [
        halo(3, hyq_ref.at[far, :], hyq_ext.at[pl.ds(NEAR + count, FAR), :], down),
        halo(4, cot_ref.at[far, :], cot_ext.at[pl.ds(count, FAR), :], down),
        halo(5, q_ref.at[near, :], q_ext.at[pl.ds(FAR + count, NEAR), :], down),
        halo(6, hyk_ref.at[near, :], hyk_ext.at[pl.ds(FAR + count, NEAR), :], down),
        halo(7, k_ref.at[near, :], aft_kv.at[0], down),
        halo(8, v_ref.at[near, :], aft_kv.at[1], down),
    ]

    def kv_copy(half, slot, target, sem):
        return pltpu.make_async_remote_copy(
            src_ref=kv.at[half, slot],
            dst_ref=kv.at[half, slot],
            send_sem=sem,
            recv_sem=kv_recv.at[half, slot],
            device_id={"ctx": target},
            device_id_type=MESH,
        )

    square = chips == 4

    def each_own(act):
        def one(d, c):
            for half in range(2):
                act(kv_copy(half, me, me + 2 * d, kv_send.at[half, d]))
            return c

        if square:

            @pl.when(chip != 1)
            def _():
                lax.fori_loop(1, jnp.minimum(chips - chip, 3), one, 0)

            @pl.when(chip == 1)
            def _():
                one(2, 0)
        else:
            lax.fori_loop(1, chips - chip, one, 0)

    def each_relay(half, earlier, act):
        if not square:
            return

        @pl.when((chip == 1 + half) & (earlier == 0))
        def _():
            act(kv_copy(half, core, 6 + core, relay_send.at[half]))

        @pl.when((chip == 3) & (earlier == 1))
        def _():
            act(kv_copy(half, 2 + core, 4 + core, relay_send.at[half]))

    def source(step):
        if square:
            return lax.rem(step + jnp.where(chip == 3, 1, 0), jnp.maximum(chip, 1))
        return chip - 1 - step

    pl.semaphore_wait(barrier, n + heads - 2)
    loads[0].wait()
    loads[1].wait()

    @pl.when(me < n - 1)
    def _():
        for copy in onward:
            copy.start()

    @pl.when(me > 0)
    def _():
        for copy in back:
            copy.start()

    each_own(lambda copy: copy.start())

    @pl.when(core == 0)
    def _():
        for half in range(2):
            kv_copy(half, me, sibling, sib_send.at[half]).start()

    @pl.when(me == 0)
    def _():
        q_ext[0:FAR, :] = jnp.zeros((FAR, HD), BF16)
        hyk_ext[0:FAR, :] = jnp.zeros((FAR, HD), BF16)
        hyq_ext[0:NEAR, :] = jnp.zeros((NEAR, HD), BF16)

    @pl.when(me == n - 1)
    def _():
        hyq_ext[NEAR + count : NEAR + count + FAR, :] = jnp.zeros((FAR, HD), BF16)
        cot_ext[count : count + FAR, :] = jnp.zeros((FAR, HD), BF16)
        q_ext[FAR + count :, :] = jnp.zeros((NEAR, HD), BF16)
        hyk_ext[FAR + count :, :] = jnp.zeros((NEAR, HD), BF16)
        aft_kv[...] = jnp.zeros(aft_kv.shape, BF16)

    loads[2].wait()

    tap = lax.broadcasted_iota(jnp.int32, (FILT, 2 * FILT), 0)
    col = lax.broadcasted_iota(jnp.int32, (FILT, 2 * FILT), 1)
    taps16 = mr_ref[...].astype(BF16)
    for out_taps, place in ((taps_b, tap == col), (taps_f, tap == FILT - col)):
        line = jnp.dot(taps16, place.astype(F32).astype(BF16), preferred_element_type=F32)
        for g in range(groups):
            spread = jnp.broadcast_to(line[g : g + 1, :], (FILT, 2 * FILT))
            moved = pltpu.roll(spread, 0, 1, stride=1, stride_axis=0)
            out_taps[g * FILT : (g + 1) * FILT, :] = moved.astype(BF16)

    scale = math.log2(math.e) / math.sqrt(HD)
    over_last = (((1,), (1,)), ((), ()))

    def attend(start, size, keys, values, key_base, masked):
        part = pl.ds(start, size)
        scores = lax.dot_general(q_ext[part, :], keys, over_last, preferred_element_type=F32)
        if masked:
            row = lax.broadcasted_iota(jnp.int32, scores.shape, 0) + (start - FAR)
            at = lax.broadcasted_iota(jnp.int32, scores.shape, 1) + key_base
            scores = jnp.where(at <= row, scores, NEGATIVE)
        old = m_ref[part, :]
        new = jnp.maximum(old, jnp.max(scores, axis=1, keepdims=True))
        m_ref[part, :] = new
        factor = jnp.exp2((old - new) * scale)
        probs = jnp.exp2((scores - new[:, 0:1]) * scale)
        if probs.shape[1] >= HD:
            sums = probs[:, :HD]
            for begin in range(HD, probs.shape[1], HD):
                sums = sums + probs[:, begin : begin + HD]
        else:
            lane0 = lax.broadcasted_iota(jnp.int32, (size, HD), 1) == 0
            sums = jnp.where(lane0, jnp.sum(probs, axis=1, keepdims=True), 0.0)
        l_ref[part, :] = l_ref[part, :] * factor + sums
        acc_ref[part, :] = acc_ref[part, :] * factor + jnp.dot(
            probs.astype(BF16), values, preferred_element_type=F32
        )

    m_ref[...] = jnp.full(m_ref.shape, NEGATIVE, F32)
    l_ref[...] = jnp.zeros(l_ref.shape, F32)
    acc_ref[...] = jnp.zeros(acc_ref.shape, F32)

    @pl.when(me > 0)
    def _():
        for copy in onward:
            copy.wait_recv()

    @pl.when(me < n - 1)
    def _():
        for copy in back:
            copy.wait_recv()

    for load in loads[3:]:
        load.wait()
    attend(0, rows, kv[0, me], kv[1, me], 0, True)
    attend(FAR + count, NEAR, aft_kv[0], aft_kv[1], count, True)

    lane_group = lax.broadcasted_iota(jnp.int32, (1, HD), 1) // GROUP_CH
    ext = 384 + NEAR
    x32[...] = hyq_ext[...].astype(F32)
    qf = taps_sum(x32, NEAR, ext, fw_ref[0], -1).astype(BF16).astype(F32)
    d_signal = (cot_ext[...].astype(F32) * qf).astype(BF16)
    win_b[0:ext, :] = d_signal
    win_b[ext:, :] = jnp.zeros((512 - ext, HD), BF16)
    win_f[ext:, :] = jnp.zeros((512 - ext, HD), BF16)
    y32[...] = hyk_ext[...].astype(F32)
    kf = taps_sum(y32, NEAR, ext, fw_ref[1], -1).astype(BF16).astype(F32)
    near_rows = count + NEAR
    d_mixed = band_product(taps_b, win_b, groups, lane_group)
    dv32[...] = (d_mixed * kf[FILT : FILT + near_rows]).astype(BF16).astype(F32)
    stage[3] = taps_sum(dv32, 0, count, fw_ref[2], 1).astype(BF16)
    stores = [
        pltpu.make_async_copy(stage.at[i], packed_ref.at[i], out_sem.at[i]) for i in range(4)
    ]
    stores[3].start()
    dk32[...] = d_mixed

    @pl.when(core == 1)
    def _():
        for half in range(2):
            kv_copy(half, sibling, sibling, sib_send.at[half]).wait_recv()
        attend(0, rows, kv[0, sibling], kv[1, sibling], -count, True)

    def bring(step):
        earlier = source(step)
        slot = 2 * earlier + core
        for half in range(2):
            kv_copy(half, slot, sibling, fwd_send.at[half, earlier]).wait_recv()
            each_relay(half, earlier, lambda copy: copy.start())
            kv_copy(half, slot, sibling, fwd_send.at[half, earlier]).start()

    def use(step):
        earlier = source(step)
        slot = 2 * earlier + 1 - core
        for half in range(2):
            kv_copy(half, slot, sibling, fwd_send.at[half, earlier]).wait_recv()
        keys = kv[0, pl.ds(2 * earlier, 2)].reshape(2 * count, HD)
        values = kv[1, pl.ds(2 * earlier, 2)].reshape(2 * count, HD)
        attend(0, rows, keys, values, (2 * earlier - me) * count, True)

    @pl.when(chip > 0)
    def _():
        bring(0)

    def remote(step, c):
        bring(step)
        use(step - 1)
        return c

    lax.fori_loop(1, chip, remote, 0)

    @pl.when(chip > 0)
    def _():
        use(chip - 1)

    total = jnp.sum(l_ref[...], axis=1, keepdims=True)
    attended = (acc_ref[...] / total).astype(BF16).astype(F32)
    squares[head] = jnp.zeros((1, 512), F32)
    squares[head, :, 0:rows] = lax.dot_general(
        jnp.ones((8, HD), F32),
        attended * attended,
        over_last,
        precision=lax.Precision.HIGHEST,
        preferred_element_type=F32,
    )[0:1]

    def sq_copy(d):
        return pltpu.make_async_remote_copy(
            src_ref=squares.at[head],
            dst_ref=squares.at[head],
            send_sem=sq_send.at[d],
            recv_sem=sq_recv.at[d],
            device_id={"head": lax.rem(head + d, heads)},
            device_id_type=MESH,
        )

    for d in range(1, heads):
        sq_copy(d).start()
    for d in range(1, heads):
        sq_copy(d).wait_recv()
    whole = squares[0]
    for other in range(1, heads):
        whole = whole + squares[other]
    mean_sq = lax.dot_general(
        jnp.broadcast_to(whole, (8, 512)),
        jnp.full((8, HD), 1.0 / (8 * width), F32),
        (((0,), (0,)), ((), ())),
        precision=lax.Precision.HIGHEST,
        preferred_element_type=F32,
    )[0:rows]
    value = (attended * lax.rsqrt(mean_sq + EPSILON) * gain_ref[...]).astype(BF16).astype(F32)
    place = lax.broadcasted_iota(jnp.int32, value.shape, 0) + (me * count - FAR)
    x32[...] = jnp.where((place >= 0) & (place < n * count), value, 0.0)
    vf = taps_sum(x32, NEAR, ext, fw_ref[2], -1).astype(BF16).astype(F32)
    win_f[0:ext, :] = (kf * vf).astype(BF16)
    signal = band_product(taps_f, win_f, groups, lane_group)
    stage[0] = (qf[0:count] * signal[0:count]).astype(BF16)
    stores[0].start()
    dq32[...] = (cot_ext[0:near_rows, :].astype(F32) * signal).astype(BF16).astype(F32)
    stage[1] = taps_sum(dq32, 0, count, fw_ref[0], 1).astype(BF16)
    stores[1].start()
    dk32[...] = (dk32[...] * vf[FILT : FILT + near_rows]).astype(BF16).astype(F32)
    stage[2] = taps_sum(dk32, 0, count, fw_ref[1], 1).astype(BF16)
    stores[2].start()

    @pl.when(me < n - 1)
    def _():
        for copy in onward:
            copy.wait_send()

    @pl.when(me > 0)
    def _():
        for copy in back:
            copy.wait_send()

    @pl.when(core == 0)
    def _():
        for half in range(2):
            kv_copy(half, me, sibling, sib_send.at[half]).wait_send()

    each_own(lambda copy: copy.wait_send())

    def sent_on(earlier, c):
        for half in range(2):
            kv_copy(half, 2 * earlier + core, sibling, fwd_send.at[half, earlier]).wait_send()
            each_relay(half, earlier, lambda copy: copy.wait_send())
        return c

    lax.fori_loop(0, chip, sent_on, 0)
    for d in range(1, heads):
        sq_copy(d).wait_send()
    for store in stores:
        store.wait()


def unpack(packed_ref, out_ref, gq_ref, gk_ref, gv_ref, stage, in_sems, sems):
    loads = [
        pltpu.make_async_copy(packed_ref.at[i], stage.at[i], in_sems.at[i]) for i in range(4)
    ]
    copies = [
        pltpu.make_async_copy(stage.at[i], dst, sems.at[i])
        for i, dst in enumerate((out_ref, gq_ref, gk_ref, gv_ref))
    ]
    for load in loads:
        load.start()
    for load, copy in zip(loads, copies):
        load.wait()
        copy.start()
    for copy in copies:
        copy.wait()


def per_device(q_att, k_att, v_att, norm_gain, hy_q, hy_k, feat_w, mr_filt, cotangent):
    count, channels = q_att.shape
    n = lax.axis_size("ctx")
    heads = lax.axis_size("head")
    groups = mr_filt.shape[1]
    depth = feat_w.shape[0]
    rows = FAR + count + NEAR
    block = jax.ShapeDtypeStruct((count, channels), BF16)
    dma = pltpu.SemaphoreType.DMA
    near_rows = count + NEAR
    hbm = pl.BlockSpec(memory_space=pltpu.HBM)
    packed = pl.pallas_call(
        functools.partial(kernel, n, heads, channels * heads),
        out_shape=jax.ShapeDtypeStruct((4, count, channels), BF16),
        in_specs=[hbm] * 9,
        out_specs=hbm,
        scratch_shapes=[
            pltpu.VMEM((2, n, count, HD), BF16),
            pltpu.VMEM((rows, HD), BF16),
            pltpu.VMEM((2, NEAR, HD), BF16),
            pltpu.VMEM((rows, HD), BF16),
            pltpu.VMEM((rows, HD), BF16),
            pltpu.VMEM((count + FAR, HD), BF16),
            pltpu.VMEM((heads, 1, 512), F32),
            pltpu.VMEM((groups * FILT, 2 * FILT), BF16),
            pltpu.VMEM((groups * FILT, 2 * FILT), BF16),
            pltpu.VMEM((512, HD), BF16),
            pltpu.VMEM((512, HD), BF16),
            pltpu.VMEM((rows, HD), F32),
            pltpu.VMEM((rows, HD), F32),
            pltpu.VMEM((rows, HD), F32),
            pltpu.VMEM((rows, HD), F32),
            pltpu.VMEM((rows, HD), F32),
            pltpu.VMEM((near_rows, HD), F32),
            pltpu.VMEM((near_rows, HD), F32),
            pltpu.VMEM((near_rows, HD), F32),
            pltpu.VMEM((1, HD), F32),
            pltpu.VMEM((depth, FEAT, HD), F32),
            pltpu.VMEM((groups, FILT), F32),
            pltpu.VMEM((4, count, HD), BF16),
            dma((9,)),
            dma((4,)),
            dma((9,)),
            dma((9,)),
            dma((2, n // 2)),
            dma((2, n // 2)),
            dma((2,)),
            dma((2, n)),
            dma((2,)),
            dma((heads,)),
            dma((heads,)),
        ],
        compiler_params=pltpu.CompilerParams(
            collective_id=0, has_side_effects=True, vmem_limit_bytes=63 * 1024 * 1024
        ),
    )(q_att, k_att, v_att, norm_gain.reshape(1, channels), hy_q, hy_k, feat_w, mr_filt.T, cotangent)
    return pl.pallas_call(
        unpack,
        out_shape=(block,) * 4,
        in_specs=[hbm],
        out_specs=(hbm,) * 4,
        scratch_shapes=[pltpu.VMEM((4, count, channels), BF16), dma((4,)), dma((4,))],
        compiler_params=pltpu.CompilerParams(vmem_limit_bytes=63 * 1024 * 1024),
    )(packed)


def solution(mesh):
    placed = (
        P("ctx", "head"),
        P("ctx", "head"),
        P("ctx", "head"),
        P("head"),
        P("ctx", "head"),
        P("ctx", "head"),
        P(None, None, "head"),
        P(None, "head"),
        P("ctx", "head"),
    )
    return jax.shard_map(
        per_device,
        mesh=mesh,
        in_specs=placed,
        out_specs=(P("ctx", "head"),) * 4,
        check_vma=False,
    )
```
